256 devices in a mesh: row: 16 (over y, z_lo), col: 16 (over x, z_hi, core).
Axes of the slice: x: 4, y: 4, z: 8 (z_hi: 2, z_lo: 4; z = z_hi * 4 + z_lo), core: 2. Of those that a mesh axis runs over, the one named last changes fastest.
Arguments:
- momentum: bfloat16 [5376, 10240], P('row', 'col'), may hold values from -6 to 6
Outputs:
- update: bfloat16 [5376, 10240], P('row', 'col')
The draws below stay inside these ranges and needn't reach their ends.
All inputs are finite; a program needn't handle non-finite values.
Results may differ from the reference program's by a relative error of at most 0.0059.
Values may be sent and summed in bfloat16 or wider, within the bound.
No kernel may reach another device: no remote copies, remote signals or barrier semaphores. Data moves between devices by JAX's collectives and lax.ppermute only.
A program may use at most 64 MiB of HBM per device.

```python
import math
import jax
import jax.numpy as jnp

R = 5376
C = 10240


def draw_momentum(key, part):
    key = jax.random.fold_in(key, 7)
    keys = jax.random.split(key, 3)
    base = jnp.clip(jax.random.normal(keys[0], (R, C), jnp.float32), -5.0, 5.0)
    row_spread = math.log(2.0)
    col_spread = math.log(2.0)
    row_norm = math.sqrt(2.0 * row_spread / (math.exp(2.0 * row_spread) - 1.0))
    col_norm = math.sqrt(2.0 * col_spread / (math.exp(2.0 * col_spread) - 1.0))
    row_scale = jnp.exp(jax.random.uniform(keys[1], (R, 1), jnp.float32) * row_spread) * row_norm
    col_scale = jnp.exp(jax.random.uniform(keys[2], (1, C), jnp.float32) * col_spread) * col_norm
    values = 0.6 * base * row_scale * col_scale
    return values.astype(jnp.bfloat16)


def setup_inputs(seed: int = 0) -> dict:
    key_list = jax.random.split(jax.random.key(seed), 2)
    return {
        "momentum": draw_momentum(jax.random.fold_in(key_list[1], 71), 0),
    }


coef_a = 3.4445
coef_b = -4.7750
coef_c = 2.0315


def reference(momentum):
    widened = momentum.astype(jnp.float32)
    gram = jnp.dot(momentum, momentum.T, preferred_element_type=jnp.float32)
    gram_scaled = (gram / C).astype(jnp.bfloat16)
    squared = jnp.dot(gram_scaled, gram_scaled, preferred_element_type=jnp.float32)
    poly = (coef_b * gram_scaled.astype(jnp.float32) + coef_c * squared).astype(jnp.bfloat16)
    product = jnp.dot(poly, momentum, preferred_element_type=jnp.float32)
    return (coef_a * widened + product).astype(jnp.bfloat16)
```

```python
import jax
import jax.numpy as jnp
from jax import lax
from jax.sharding import Mesh, PartitionSpec as P

C = 10240
B = 336

coef_a = 3.4445
coef_b = -4.775
coef_c = 2.0315

AXES = ("y", "zl", "x", "zh", "core")


def send_xor(v, axis, size, k):
    return lax.ppermute(v, axis, [(i, i ^ k) for i in range(size)])


def send_up(v, axis, size, k):
    return lax.ppermute(v, axis, [(i, (i + k) % size) for i in range(size)])


def gather_z(v):
    return jnp.concatenate([v] + [send_xor(v, "zl", 4, t) for t in (1, 2, 3)], axis=0)


def gather_y(v):
    return jnp.concatenate([v] + [send_up(v, "y", 4, -s) for s in (1, 2, 3)], axis=0)


def reduce_y(partial):
    total = partial[:B]
    sent = partial.astype(jnp.bfloat16)
    for s in (1, 2, 3):
        total = total + send_up(sent[s * B : (s + 1) * B], "y", 4, s).astype(jnp.float32)
    return total


def body(momentum):
    core = lax.axis_index("core")
    xi = lax.axis_index("x")
    half, quarter = 2 * B, B // 2
    x2 = gather_z(momentum)
    x1 = gather_y(momentum)
    partial = lax.dot_general(
        x1, x2, (((1,), (1,)), ((), ())), preferred_element_type=jnp.float32
    )
    kept = lax.dynamic_slice_in_dim(partial, core * half, half, 0)
    given = lax.dynamic_slice_in_dim(partial, (1 - core) * half, half, 0)
    got = send_xor(given.astype(jnp.bfloat16), "core", 2, 1)
    chip = kept + got.astype(jnp.float32)
    chip_sent = chip.astype(jnp.bfloat16)
    total = lax.dynamic_slice_in_dim(chip, xi * quarter, quarter, 0)
    for k in (1, 2, 3):
        piece = lax.dynamic_slice_in_dim(chip_sent, (xi ^ k) * quarter, quarter, 0)
        total = total + send_xor(piece, "x", 4, k).astype(jnp.float32)
    total = total + send_xor(total.astype(jnp.bfloat16), "zh", 2, 1).astype(jnp.float32)
    mine = (total / C).astype(jnp.bfloat16)
    rows = jnp.zeros((half, 4 * B), jnp.bfloat16)
    rows = lax.dynamic_update_slice_in_dim(rows, mine, xi * quarter, 0)
    for k in (1, 2, 3):
        rows = lax.dynamic_update_slice_in_dim(
            rows, send_xor(mine, "x", 4, k), (xi ^ k) * quarter, 0
        )
    other = send_xor(rows, "core", 2, 1)
    gram = jnp.zeros((4 * B, 4 * B), jnp.bfloat16)
    gram = lax.dynamic_update_slice_in_dim(gram, rows, core * half, 0)
    gram = lax.dynamic_update_slice_in_dim(gram, other, (1 - core) * half, 0)
    first = reduce_y(jnp.dot(gram, x2, preferred_element_type=jnp.float32))
    y2 = gather_z(first.astype(jnp.bfloat16))
    second = reduce_y(jnp.dot(gram, y2, preferred_element_type=jnp.float32))
    return (
        coef_a * momentum.astype(jnp.float32) + coef_b * first + coef_c * second
    ).astype(jnp.bfloat16)


def solution(mesh):
    fine = Mesh(mesh.devices.reshape(4, 4, 4, 2, 2), AXES)
    spec = P(("y", "zl"), ("x", "zh", "core"))
    return jax.shard_map(body, mesh=fine, in_specs=(spec,), out_specs=spec, check_vma=False)
```

```python
import jax
import jax.numpy as jnp
from jax import lax
from jax.sharding import Mesh, PartitionSpec as P

C = 10240
B = 336
G = 384

coef_a = 3.4445
coef_b = -4.775
coef_c = 2.0315

AXES = ("y", "zl", "x", "zh", "core")
OFFSETS = (1, 2, 3)


def send_xor(v, axis, size, k):
    return lax.ppermute(v, axis, [(i, i ^ k) for i in range(size)])


def send_up(v, axis, size, k):
    return lax.ppermute(v, axis, [(i, (i + k) % size) for i in range(size)])


def wide(v):
    return v.astype(jnp.float32)


def narrow(v):
    return v.astype(jnp.bfloat16)


def rows_dot(a, b):
    return lax.dot_general(a, b, (((1,), (1,)), ((), ())), preferred_element_type=jnp.float32)


def gather_z(v):
    return jnp.concatenate([v] + [send_xor(v, "zl", 4, t) for t in OFFSETS], axis=0)


def gather_y(v):
    return jnp.concatenate([v] + [send_up(v, "y", 4, -s) for s in OFFSETS], axis=0)


def reduce_y(partial):
    total = partial[:B]
    sent = narrow(partial)
    for s in OFFSETS:
        total = total + wide(send_up(sent[s * B : (s + 1) * B], "y", 4, s))
    return total


def reduce_z(partial):
    total = partial[:B]
    sent = narrow(partial)
    for t in OFFSETS:
        total = total + wide(send_xor(sent[t * B : (t + 1) * B], "zl", 4, t))
    return total


def gram_chunk(low, high, x1, core, xi):
    kept = jnp.where(core == 0, low, high)
    given = jnp.where(core == 0, high, low)
    got = send_xor(narrow(rows_dot(given, x1)), "core", 2, 1)
    chip = (rows_dot(kept, x1) + wide(got)).reshape(4, B // 4, 4 * B)
    sent = narrow(chip)
    total = lax.dynamic_index_in_dim(chip, xi, 0, keepdims=False)
    for k in OFFSETS:
        piece = lax.dynamic_index_in_dim(sent, xi ^ k, 0, keepdims=False)
        total = total + wide(send_xor(piece, "x", 4, k))
    total = total + wide(send_xor(narrow(total), "zh", 2, 1))
    mine = narrow(total / C)
    rows = jnp.zeros((4, B // 4, 4 * B), jnp.bfloat16)
    rows = lax.dynamic_update_index_in_dim(rows, mine, xi, 0)
    for k in OFFSETS:
        rows = lax.dynamic_update_index_in_dim(rows, send_xor(mine, "x", 4, k), xi ^ k, 0)
    rows = rows.reshape(B, 4 * B)
    other = send_xor(rows, "core", 2, 1)
    first = jnp.where(core == 0, rows, other)
    last = jnp.where(core == 0, other, rows)
    return [first, last]


def body(momentum):
    core = lax.axis_index("core")
    xi = lax.axis_index("x")
    z = [momentum] + [send_xor(momentum, "zl", 4, t) for t in OFFSETS]
    x1 = gather_y(momentum)
    x2 = jnp.concatenate(z, axis=0)
    gram = jnp.concatenate(
        gram_chunk(z[0], z[1], x1, core, xi) + gram_chunk(z[2], z[3], x1, core, xi), axis=0
    )

    def over_y(v):
        return lax.dot_general(
            gram, v, (((0,), (0,)), ((), ())), preferred_element_type=jnp.float32
        )

    first_l = reduce_y(over_y(x2[:, :G]))
    first_r = reduce_y(over_y(x2[:, G:]))
    second_l = reduce_y(over_y(gather_z(narrow(first_l))))
    second_r = reduce_z(
        jnp.dot(gram, gather_y(narrow(first_r)), preferred_element_type=jnp.float32)
    )
    m = wide(momentum)
    out_l = coef_a * m[:, :G] + coef_b * first_l + coef_c * second_l
    out_r = coef_a * m[:, G:] + coef_b * first_r + coef_c * second_r
    return narrow(jnp.concatenate([out_l, out_r], axis=1))


def solution(mesh):
    fine = Mesh(mesh.devices.reshape(4, 4, 4, 2, 2), AXES)
    spec = P(("y", "zl"), ("x", "zh", "core"))
    return jax.shard_map(body, mesh=fine, in_specs=(spec,), out_specs=spec, check_vma=False)
```

```python
import jax
import jax.numpy as jnp
from jax import lax
from jax.sharding import Mesh, PartitionSpec as P

C = 10240
B = 336
H = 168
G = 384
CUT = 640

coef_a = 3.4445
coef_b = -4.775
coef_c = 2.0315

AXES = ("y", "zl", "x", "zh", "core")
OFFSETS = (1, 2, 3)


def send_xor(v, axis, size, k):
    return lax.ppermute(v, axis, [(i, i ^ k) for i in range(size)])


def send_up(v, axis, size, k):
    return lax.ppermute(v, axis, [(i, (i + k) % size) for i in range(size)])


def wide(v):
    return v.astype(jnp.float32)


def narrow(v):
    return v.astype(jnp.bfloat16)


def dot(a, b, da, db):
    return lax.dot_general(a, b, (((da,), (db,)), ((), ())), preferred_element_type=jnp.float32)


def gather_z(v):
    return jnp.concatenate([v] + [send_xor(v, "zl", 4, t) for t in OFFSETS], axis=0)


def gather_y(v):
    return jnp.concatenate([v] + [send_up(v, "y", 4, -s) for s in OFFSETS], axis=0)


def reduce_y(partial):
    total = partial[:B]
    sent = narrow(partial)
    for s in OFFSETS:
        total = total + wide(send_up(sent[s * B : (s + 1) * B], "y", 4, s))
    return total


def reduce_z(partial):
    total = partial[:B]
    sent = narrow(partial)
    for t in OFFSETS:
        total = total + wide(send_xor(sent[t * B : (t + 1) * B], "zl", 4, t))
    return total


def chip_chunk(kept, given, x2):
    got = send_xor(narrow(dot(given, x2, 1, 1)), "core", 2, 1)
    return narrow(dot(kept, x2, 1, 1) + wide(got)).reshape(4, H, x2.shape[0])


def gram_chunk(chip, xi):
    total = wide(lax.dynamic_index_in_dim(chip, xi, 0, keepdims=False))
    for k in OFFSETS:
        piece = lax.dynamic_index_in_dim(chip, xi ^ k, 0, keepdims=False)
        total = total + wide(send_xor(piece, "x", 4, k))
    total = total + wide(send_xor(narrow(total), "zh", 2, 1))
    mine = narrow(total / C)
    rows = jnp.zeros(chip.shape, jnp.bfloat16)
    rows = lax.dynamic_update_index_in_dim(rows, mine, xi, 0)
    for k in OFFSETS:
        rows = lax.dynamic_update_index_in_dim(rows, send_xor(mine, "x", 4, k), xi ^ k, 0)
    return rows, send_xor(rows, "core", 2, 1)


def body(momentum):
    core = lax.axis_index("core")
    xi = lax.axis_index("x")
    z2 = send_xor(momentum, "zl", 4, 2)
    z3 = send_xor(momentum, "zl", 4, 3)
    y1 = send_up(momentum, "y", 4, -1)
    later, y1 = lax.optimization_barrier((momentum, y1))
    z1 = send_xor(later, "zl", 4, 1)
    y2 = send_up(momentum, "y", 4, -2)
    y3 = send_up(momentum, "y", 4, -3)
    x1 = jnp.concatenate([momentum, y1, y2, y3], axis=0)
    halves = x1.reshape(4, 2, H, -1)
    kept = jnp.where(core == 0, halves[:, 0], halves[:, 1]).reshape(2 * B, -1)
    given = jnp.where(core == 0, halves[:, 1], halves[:, 0]).reshape(2 * B, -1)
    chip_a = chip_chunk(kept, given, jnp.concatenate([momentum, z1[: CUT - B]], axis=0))
    chip_b = chip_chunk(kept, given, jnp.concatenate([z1[CUT - B :], z2, z3], axis=0))
    gram = jnp.zeros((4, 2, H, 4 * B), jnp.bfloat16)
    for chip, place in ((chip_a, 0), (chip_b, CUT)):
        rows, other = gram_chunk(chip, xi)
        gram = lax.dynamic_update_slice(gram, rows[:, None], (0, core, 0, place))
        gram = lax.dynamic_update_slice(gram, other[:, None], (0, 1 - core, 0, place))
    gram = gram.reshape(4 * B, 4 * B)
    x2 = jnp.concatenate([momentum, z1, z2, z3], axis=0)
    first = reduce_y(dot(gram, x2, 1, 0))
    first_n = narrow(first)
    second_l = reduce_y(dot(gram, gather_z(first_n[:, :G]), 1, 0))
    second_r = reduce_z(dot(gram, gather_y(first_n[:, G:]), 0, 0))
    second = jnp.concatenate([second_l, second_r], axis=1)
    return narrow(coef_a * wide(momentum) + coef_b * first + coef_c * second)


def solution(mesh):
    fine = Mesh(mesh.devices.reshape(4, 4, 4, 2, 2), AXES)
    spec = P(("y", "zl"), ("x", "zh", "core"))
    return jax.shard_map(body, mesh=fine, in_specs=(spec,), out_specs=spec, check_vma=False)
```

```python
import jax
import jax.numpy as jnp
from jax import lax
from jax.sharding import Mesh, PartitionSpec as P

C = 10240
B = 336
H = 168
G = 384
CUT = 640

coef_a = 3.4445
coef_b = -4.775
coef_c = 2.0315

AXES = ("y", "zl", "x", "zh", "core")
OFFSETS = (1, 2, 3)


def send_xor(v, axis, size, k):
    return lax.ppermute(v, axis, [(i, i ^ k) for i in range(size)])


def send_up(v, axis, size, k):
    return lax.ppermute(v, axis, [(i, (i + k) % size) for i in range(size)])


def wide(v):
    return v.astype(jnp.float32)


def narrow(v):
    return v.astype(jnp.bfloat16)


def dot(a, b, da, db):
    return lax.dot_general(a, b, (((da,), (db,)), ((), ())), preferred_element_type=jnp.float32)


def gather_z(v):
    return jnp.concatenate([v] + [send_xor(v, "zl", 4, t) for t in OFFSETS], axis=0)


def gather_y(v):
    return jnp.concatenate([v] + [send_up(v, "y", 4, -s) for s in OFFSETS], axis=0)


def reduce_y(partial):
    total = partial[:B]
    sent = narrow(partial)
    for s in OFFSETS:
        total = total + wide(send_up(sent[s * B : (s + 1) * B], "y", 4, s))
    return total


def reduce_z(partial):
    total = partial[:B]
    sent = narrow(partial)
    for t in OFFSETS:
        total = total + wide(send_xor(sent[t * B : (t + 1) * B], "zl", 4, t))
    return total


def swap(v):
    return send_xor(v, "core", 2, 1)


def pick(core, v):
    return jnp.where(core == 0, v[:H], v[H:])


def sum_x(chip, xi):
    total = wide(lax.dynamic_index_in_dim(chip, xi, 0, keepdims=False))
    for k in OFFSETS:
        piece = lax.dynamic_index_in_dim(chip, xi ^ k, 0, keepdims=False)
        total = total + wide(send_xor(piece, "x", 4, k))
    return total


def gram_chunk(total, xi):
    total = total + wide(send_xor(narrow(total), "zh", 2, 1))
    mine = narrow(total / C)
    rows = jnp.zeros((4,) + mine.shape, jnp.bfloat16)
    rows = lax.dynamic_update_index_in_dim(rows, mine, xi, 0)
    for k in OFFSETS:
        rows = lax.dynamic_update_index_in_dim(rows, send_xor(mine, "x", 4, k), xi ^ k, 0)
    return rows, swap(rows)


def body(momentum):
    core = lax.axis_index("core")
    xi = lax.axis_index("x")
    zl = lax.axis_index("zl")
    down1 = lax.ppermute(momentum, "zl", [(1, 0), (2, 1), (3, 2)])
    up1 = lax.ppermute(momentum, "zl", [(0, 1), (1, 2), (2, 3)])
    y1 = send_up(momentum, "y", 4, -1)
    y3 = send_up(momentum, "y", 4, 1)
    down1, up1, y1, y3 = lax.optimization_barrier((down1, up1, y1, y3))
    down2 = lax.ppermute(down1, "zl", [(1, 0), (2, 1)])
    up2 = lax.ppermute(up1, "zl", [(1, 2), (2, 3)])
    y2 = send_up(y1, "y", 4, -1)
    down2, up2, y2 = lax.optimization_barrier((down2, up2, y2))
    end = lax.ppermute(jnp.where(zl == 1, down2, up2), "zl", [(1, 0), (2, 3)])
    z1 = jnp.where(zl % 2 == 0, down1, up1)
    z2 = jnp.where(zl < 2, down2, up2)
    y = [y1, y2, y3]
    m_o = swap(momentum)
    rows = [jnp.concatenate([pick(core, momentum), pick(core, m_o)], axis=1)]
    rows += [jnp.concatenate([pick(core, v), swap(pick(1 - core, v))], axis=1) for v in y]
    rows = jnp.concatenate(rows, axis=0)
    z0, z1w = (
        jnp.concatenate([v, o], axis=1) for v, o in ((momentum, m_o), (z1, swap(z1)))
    )

    def chip_chunk(blocks):
        x2 = jnp.concatenate(blocks, axis=0)
        return narrow(dot(rows, x2, 1, 1)).reshape(4, H, x2.shape[0])

    sum_a = sum_x(chip_chunk([z0, z1w[: CUT - B]]), xi)
    end, sum_a = lax.optimization_barrier((end, sum_a))
    z3 = jnp.where(zl == 1, down1, jnp.where(zl == 2, up1, end))
    z2w, z3w = (jnp.concatenate([v, swap(v)], axis=1) for v in (z2, z3))
    sum_b = sum_x(chip_chunk([z1w[CUT - B :], z2w, z3w]), xi)
    gram = jnp.zeros((4, 2, H, 4 * B), jnp.bfloat16)
    for total, place in ((sum_a, 0), (sum_b, CUT)):
        rows, other = gram_chunk(total, xi)
        gram = lax.dynamic_update_slice(gram, rows[:, None], (0, core, 0, place))
        gram = lax.dynamic_update_slice(gram, other[:, None], (0, 1 - core, 0, place))
    gram = gram.reshape(4 * B, 4 * B)
    x2 = jnp.concatenate([momentum, z1, z2, z3], axis=0)
    first_l = reduce_y(dot(gram, x2[:, :G], 1, 0))
    x2_r, _ = lax.optimization_barrier((x2[:, G:], first_l))
    first_r = reduce_y(dot(gram, x2_r, 1, 0))
    second_l = reduce_y(dot(gram, gather_z(narrow(first_l)), 1, 0))
    second_r = reduce_z(dot(gram, gather_y(narrow(first_r)), 0, 0))
    m = wide(momentum)
    out_l = coef_a * m[:, :G] + coef_b * first_l + coef_c * second_l
    out_r = coef_a * m[:, G:] + coef_b * first_r + coef_c * second_r
    return narrow(jnp.concatenate([out_l, out_r], axis=1))


def solution(mesh):
    fine = Mesh(mesh.devices.reshape(4, 4, 4, 2, 2), AXES)
    spec = P(("y", "zl"), ("x", "zh", "core"))
    return jax.shard_map(body, mesh=fine, in_specs=(spec,), out_specs=spec, check_vma=False)
```

```python
import jax
import jax.numpy as jnp
from jax import lax
from jax.sharding import Mesh, PartitionSpec as P

C = 10240
B = 336
H = 168
CUT = 512

coef_a = 3.4445
coef_b = -4.775
coef_c = 2.0315

AXES = ("y", "zl", "x", "zh", "core")
OFFSETS = (1, 2, 3)


def send_xor(v, axis, size, k):
    return lax.ppermute(v, axis, [(i, i ^ k) for i in range(size)])


def send_up(v, axis, size, k):
    return lax.ppermute(v, axis, [(i, (i + k) % size) for i in range(size)])


def wide(v):
    return v.astype(jnp.float32)


def narrow(v):
    return v.astype(jnp.bfloat16)


def dot(a, b, da, db):
    return lax.dot_general(a, b, (((da,), (db,)), ((), ())), preferred_element_type=jnp.float32)


def swap(v):
    return send_xor(v, "core", 2, 1)


def pick(core, v):
    return jnp.where(core == 0, v[:H], v[H:])


SLOT_A = [(1, 0), (3, 1), (0, 2), (2, 3)]
SLOT_B = [(3, 0), (1, 2)]


def fetch_z(v):
    return [lax.ppermute(v, "zl", SLOT_A), lax.ppermute(v, "zl", SLOT_B)]


def fetch_y(v):
    return [send_up(v, "y", 4, -s) for s in OFFSETS]


def apply_gram(gram, columns, rows):
    part = dot(gram, columns, 1, 0)
    back = narrow(dot(gram[:, : 2 * B], rows, 0, 0))
    sent = narrow(part)
    total = part[:B]
    total = total + wide(lax.ppermute(back[:B], "zl", [(b, a) for a, b in SLOT_A]))
    total = total + wide(lax.ppermute(back[B:], "zl", [(b, a) for a, b in SLOT_B]))
    for s in OFFSETS:
        total = total + wide(send_up(sent[s * B : (s + 1) * B], "y", 4, s))
    return total


def sum_x(chip, xi):
    total = wide(lax.dynamic_index_in_dim(chip, xi, 0, keepdims=False))
    for k in OFFSETS:
        piece = lax.dynamic_index_in_dim(chip, xi ^ k, 0, keepdims=False)
        total = total + wide(send_xor(piece, "x", 4, k))
    return total


def gram_chunk(total, xi):
    total = total + wide(send_xor(narrow(total), "zh", 2, 1))
    mine = narrow(total / C)
    rows = jnp.zeros((4,) + mine.shape, jnp.bfloat16)
    rows = lax.dynamic_update_index_in_dim(rows, mine, xi, 0)
    for k in OFFSETS:
        rows = lax.dynamic_update_index_in_dim(rows, send_xor(mine, "x", 4, k), xi ^ k, 0)
    return rows, swap(rows)


def body(momentum):
    core = lax.axis_index("core")
    xi = lax.axis_index("x")
    za, zb = fetch_z(momentum)
    y = fetch_y(momentum)
    m_o = swap(momentum)
    rows = [jnp.concatenate([pick(core, momentum), pick(core, m_o)], axis=1)]
    rows += [jnp.concatenate([pick(core, v), swap(pick(1 - core, v))], axis=1) for v in y]
    rows = jnp.concatenate(rows, axis=0)
    za_w, zb_w, own_w = (
        jnp.concatenate([v, o], axis=1)
        for v, o in ((za, swap(za)), (zb, swap(zb)), (momentum, m_o))
    )

    def chip_chunk(blocks):
        columns = jnp.concatenate(blocks, axis=0)
        return narrow(dot(rows, columns, 1, 1)).reshape(4, H, columns.shape[0])

    cut = CUT - B
    sum_a = sum_x(chip_chunk([za_w, zb_w[:cut]]), xi)
    sum_b = sum_x(chip_chunk([zb_w[cut:], own_w]), xi)
    gram = jnp.zeros((4, 2, H, 3 * B), jnp.bfloat16)
    for total, place in ((sum_a, 0), (sum_b, CUT)):
        part, other = gram_chunk(total, xi)
        gram = lax.dynamic_update_slice(gram, part[:, None], (0, core, 0, place))
        gram = lax.dynamic_update_slice(gram, other[:, None], (0, 1 - core, 0, place))
    gram = gram.reshape(4 * B, 3 * B)
    columns = jnp.concatenate([za, zb, momentum], axis=0)
    first = apply_gram(gram, columns, jnp.concatenate([momentum] + y, axis=0))
    sent = narrow(first)
    columns = jnp.concatenate(fetch_z(sent) + [sent], axis=0)
    second = apply_gram(gram, columns, jnp.concatenate([sent] + fetch_y(sent), axis=0))
    return narrow(coef_a * wide(momentum) + coef_b * first + coef_c * second)


def solution(mesh):
    fine = Mesh(mesh.devices.reshape(4, 4, 4, 2, 2), AXES)
    spec = P(("y", "zl"), ("x", "zh", "core"))
    return jax.shard_map(body, mesh=fine, in_specs=(spec,), out_specs=spec, check_vma=False)
```

```python
import jax
import jax.numpy as jnp
from jax import lax
from jax.sharding import Mesh, PartitionSpec as P

C = 10240
B = 336
H = 168
CUT = 512

coef_a = 3.4445
coef_b = -4.775
coef_c = 2.0315

AXES = ("y", "zl", "x", "zh", "core")
OFFSETS = (1, 2, 3)


def send_xor(v, axis, size, k):
    return lax.ppermute(v, axis, [(i, i ^ k) for i in range(size)])


def send_up(v, axis, size, k):
    return lax.ppermute(v, axis, [(i, (i + k) % size) for i in range(size)])


def wide(v):
    return v.astype(jnp.float32)


def narrow(v):
    return v.astype(jnp.bfloat16)


def dot(a, b, da, db):
    return lax.dot_general(a, b, (((da,), (db,)), ((), ())), preferred_element_type=jnp.float32)


def swap(v):
    return send_xor(v, "core", 2, 1)


def pick(core, v):
    return jnp.where(core == 0, v[:H], v[H:])


SLOT_A = [(1, 0), (3, 1), (0, 2), (2, 3)]
SLOT_B = [(3, 0), (1, 2)]


def fetch_z(v):
    return [lax.ppermute(v, "zl", SLOT_A), lax.ppermute(v, "zl", SLOT_B)]


def fetch_y(v):
    return [send_up(v, "y", 4, -s) for s in OFFSETS]


def apply_gram(gram, columns, rows):
    part = dot(gram, columns, 1, 0)
    back = narrow(dot(gram[:, : 2 * B], rows, 0, 0))
    sent, back = lax.optimization_barrier((narrow(part), back))
    total = part[:B]
    for s in OFFSETS:
        total = total + wide(send_up(sent[s * B : (s + 1) * B], "y", 4, s))
    total = total + wide(lax.ppermute(back[:B], "zl", [(b, a) for a, b in SLOT_A]))
    total = total + wide(lax.ppermute(back[B:], "zl", [(b, a) for a, b in SLOT_B]))
    return total


def sum_x(chip, xi):
    total = wide(lax.dynamic_index_in_dim(chip, xi, 0, keepdims=False))
    for k in OFFSETS:
        piece = lax.dynamic_index_in_dim(chip, xi ^ k, 0, keepdims=False)
        total = total + wide(send_xor(piece, "x", 4, k))
    return total


def gram_chunk(total, xi):
    total = total + wide(send_xor(narrow(total), "zh", 2, 1))
    mine = narrow(total / C)
    rows = jnp.zeros((4,) + mine.shape, jnp.bfloat16)
    rows = lax.dynamic_update_index_in_dim(rows, mine, xi, 0)
    for k in OFFSETS:
        rows = lax.dynamic_update_index_in_dim(rows, send_xor(mine, "x", 4, k), xi ^ k, 0)
    return rows, swap(rows)


def body(momentum):
    core = lax.axis_index("core")
    xi = lax.axis_index("x")
    y = fetch_y(momentum)
    za, zb = fetch_z(momentum)
    m_o = swap(momentum)
    rows = [jnp.concatenate([pick(core, momentum), pick(core, m_o)], axis=1)]
    rows += [jnp.concatenate([pick(core, v), swap(pick(1 - core, v))], axis=1) for v in y]
    rows = jnp.concatenate(rows, axis=0)
    za_w, zb_w, own_w = (
        jnp.concatenate([v, o], axis=1)
        for v, o in ((za, swap(za)), (zb, swap(zb)), (momentum, m_o))
    )

    def chip_chunk(blocks):
        columns = jnp.concatenate(blocks, axis=0)
        return narrow(dot(rows, columns, 1, 1)).reshape(4, H, columns.shape[0])

    cut = CUT - B
    sum_a = sum_x(chip_chunk([za_w, zb_w[:cut]]), xi)
    sum_b = sum_x(chip_chunk([zb_w[cut:], own_w]), xi)
    gram = jnp.zeros((4, 2, H, 3 * B), jnp.bfloat16)
    for total, place in ((sum_a, 0), (sum_b, CUT)):
        part, other = gram_chunk(total, xi)
        gram = lax.dynamic_update_slice(gram, part[:, None], (0, core, 0, place))
        gram = lax.dynamic_update_slice(gram, other[:, None], (0, 1 - core, 0, place))
    gram = gram.reshape(4 * B, 3 * B)
    columns = jnp.concatenate([za, zb, momentum], axis=0)
    first = apply_gram(gram, columns, jnp.concatenate([momentum] + y, axis=0))
    sent = narrow(first)
    rows = jnp.concatenate([sent] + fetch_y(sent), axis=0)
    columns = jnp.concatenate(fetch_z(sent) + [sent], axis=0)
    second = apply_gram(gram, columns, rows)
    return narrow(coef_a * wide(momentum) + coef_b * first + coef_c * second)


def solution(mesh):
    fine = Mesh(mesh.devices.reshape(4, 4, 4, 2, 2), AXES)
    spec = P(("y", "zl"), ("x", "zh", "core"))
    return jax.shard_map(body, mesh=fine, in_specs=(spec,), out_specs=spec, check_vma=False)
```

```python
import jax
import jax.numpy as jnp
from jax import lax
from jax.sharding import Mesh, PartitionSpec as P

C = 10240
B = 336
H = 168
CUT = 512
G = 384

coef_a = 3.4445
coef_b = -4.775
coef_c = 2.0315

AXES = ("y", "zl", "x", "zh", "core")
OFFSETS = (1, 2, 3)


def send_xor(v, axis, size, k):
    return lax.ppermute(v, axis, [(i, i ^ k) for i in range(size)])


def send_up(v, axis, size, k):
    return lax.ppermute(v, axis, [(i, (i + k) % size) for i in range(size)])


def wide(v):
    return v.astype(jnp.float32)


def narrow(v):
    return v.astype(jnp.bfloat16)


def dot(a, b, da, db):
    return lax.dot_general(a, b, (((da,), (db,)), ((), ())), preferred_element_type=jnp.float32)


def swap(v):
    return send_xor(v, "core", 2, 1)


def pick(core, v):
    return jnp.where(core == 0, v[:H], v[H:])


SLOT_A = [(1, 0), (3, 1), (0, 2), (2, 3)]
SLOT_B = [(3, 0), (1, 2)]


def fetch_z(v):
    return [lax.ppermute(v, "zl", SLOT_A), lax.ppermute(v, "zl", SLOT_B)]


def fetch_y(v):
    return [send_up(v, "y", 4, -s) for s in OFFSETS]


def products(gram, columns, rows):
    part = dot(gram, columns, 1, 0)
    back = dot(gram[:, : 2 * B], rows, 0, 0)
    sent, back = lax.optimization_barrier((narrow(part), narrow(back)))
    return part[:B], sent, back


def collect(kept, sent, back):
    total = kept
    for s in OFFSETS:
        total = total + wide(send_up(sent[s * B : (s + 1) * B], "y", 4, s))
    total = total + wide(lax.ppermute(back[:B], "zl", [(b, a) for a, b in SLOT_A]))
    total = total + wide(lax.ppermute(back[B:], "zl", [(b, a) for a, b in SLOT_B]))
    return total


def sum_x(chip, xi):
    total = wide(lax.dynamic_index_in_dim(chip, xi, 0, keepdims=False))
    for k in OFFSETS:
        piece = lax.dynamic_index_in_dim(chip, xi ^ k, 0, keepdims=False)
        total = total + wide(send_xor(piece, "x", 4, k))
    return total


def gram_chunk(total, xi):
    total = total + wide(send_xor(narrow(total), "zh", 2, 1))
    mine = narrow(total / C)
    rows = jnp.zeros((4,) + mine.shape, jnp.bfloat16)
    rows = lax.dynamic_update_index_in_dim(rows, mine, xi, 0)
    for k in OFFSETS:
        rows = lax.dynamic_update_index_in_dim(rows, send_xor(mine, "x", 4, k), xi ^ k, 0)
    return rows, swap(rows)


def body(momentum):
    core = lax.axis_index("core")
    xi = lax.axis_index("x")
    y = fetch_y(momentum)
    za, zb = fetch_z(momentum)
    m_o = swap(momentum)
    rows = [jnp.concatenate([pick(core, momentum), pick(core, m_o)], axis=1)]
    rows += [jnp.concatenate([pick(core, v), swap(pick(1 - core, v))], axis=1) for v in y]
    rows = jnp.concatenate(rows, axis=0)
    za_w, zb_w, own_w = (
        jnp.concatenate([v, o], axis=1)
        for v, o in ((za, swap(za)), (zb, swap(zb)), (momentum, m_o))
    )

    def chip_chunk(blocks):
        columns = jnp.concatenate(blocks, axis=0)
        return narrow(dot(rows, columns, 1, 1)).reshape(4, H, columns.shape[0])

    cut = CUT - B
    sum_a = sum_x(chip_chunk([za_w, zb_w[:cut]]), xi)
    sum_b = sum_x(chip_chunk([zb_w[cut:], own_w]), xi)
    gram = jnp.zeros((4, 2, H, 3 * B), jnp.bfloat16)
    for total, place in ((sum_a, 0), (sum_b, CUT)):
        part, other = gram_chunk(total, xi)
        gram = lax.dynamic_update_slice(gram, part[:, None], (0, core, 0, place))
        gram = lax.dynamic_update_slice(gram, other[:, None], (0, 1 - core, 0, place))
    gram = gram.reshape(4 * B, 3 * B)
    columns = jnp.concatenate([za, zb, momentum], axis=0)
    rows = jnp.concatenate([momentum] + y, axis=0)
    right = products(gram, columns[:, G:], rows[:, G:])
    columns_l, rows_l, _ = lax.optimization_barrier((columns[:, :G], rows[:, :G], right[1]))
    left = products(gram, columns_l, rows_l)
    firsts, seconds = [], []
    for group in (left, right):
        first = collect(*group)
        firsts.append(first)
        sent = narrow(first)
        rows = jnp.concatenate([sent] + fetch_y(sent), axis=0)
        columns = jnp.concatenate(fetch_z(sent) + [sent], axis=0)
        seconds.append(collect(*products(gram, columns, rows)))
    first = jnp.concatenate(firsts, axis=1)
    second = jnp.concatenate(seconds, axis=1)
    return narrow(coef_a * wide(momentum) + coef_b * first + coef_c * second)


def solution(mesh):
    fine = Mesh(mesh.devices.reshape(4, 4, 4, 2, 2), AXES)
    spec = P(("y", "zl"), ("x", "zh", "core"))
    return jax.shard_map(body, mesh=fine, in_specs=(spec,), out_specs=spec, check_vma=False)
```

```python
import jax
import jax.numpy as jnp
from jax import lax
from jax.sharding import Mesh, PartitionSpec as P

C = 10240
B = 336
H = 168
CUT = 512

coef_a = 3.4445
coef_b = -4.775
coef_c = 2.0315

AXES = ("y", "zl", "x", "zh", "core")
OFFSETS = (1, 2, 3)


def send_xor(v, axis, size, k):
    return lax.ppermute(v, axis, [(i, i ^ k) for i in range(size)])


def send_up(v, axis, size, k):
    return lax.ppermute(v, axis, [(i, (i + k) % size) for i in range(size)])


def wide(v):
    return v.astype(jnp.float32)


def narrow(v):
    return v.astype(jnp.bfloat16)


def dot(a, b, da, db):
    return lax.dot_general(a, b, (((da,), (db,)), ((), ())), preferred_element_type=jnp.float32)


def swap(v):
    return send_xor(v, "core", 2, 1)


def pick(core, v):
    return jnp.where(core == 0, v[:H], v[H:])


SLOT_A = [(1, 0), (3, 1), (0, 2), (2, 3)]
SLOT_B = [(3, 0), (1, 2)]


def fetch_z(v):
    return [lax.ppermute(v, "zl", SLOT_A), lax.ppermute(v, "zl", SLOT_B)]


def fetch_y(v):
    return [send_up(v, "y", 4, -s) for s in OFFSETS]


def products(grams, columns, rows):
    part = dot(grams[0], columns[0], 1, 0) + dot(grams[1], columns[1], 1, 0)
    backs = [narrow(dot(gram[:, :B], rows, 0, 0)) for gram in grams]
    return part, backs


def collect(part, sent, backs):
    total = part[:B]
    for s in OFFSETS:
        total = total + wide(send_up(sent[s * B : (s + 1) * B], "y", 4, s))
    for back, slot in zip(backs, (SLOT_A, SLOT_B)):
        total = total + wide(lax.ppermute(back, "zl", [(b, a) for a, b in slot]))
    return total


def sum_x(chip, xi):
    total = wide(lax.dynamic_index_in_dim(chip, xi, 0, keepdims=False))
    for k in OFFSETS:
        piece = lax.dynamic_index_in_dim(chip, xi ^ k, 0, keepdims=False)
        total = total + wide(send_xor(piece, "x", 4, k))
    return total


def gram_chunk(total, xi):
    total = total + wide(send_xor(narrow(total), "zh", 2, 1))
    mine = narrow(total / C)
    rows = jnp.zeros((4,) + mine.shape, jnp.bfloat16)
    rows = lax.dynamic_update_index_in_dim(rows, mine, xi, 0)
    for k in OFFSETS:
        rows = lax.dynamic_update_index_in_dim(rows, send_xor(mine, "x", 4, k), xi ^ k, 0)
    return rows, swap(rows)


def body(momentum):
    core = lax.axis_index("core")
    xi = lax.axis_index("x")
    y = fetch_y(momentum)
    za, zb = fetch_z(momentum)
    m_o = swap(momentum)
    rows = [jnp.concatenate([pick(core, momentum), pick(core, m_o)], axis=1)]
    rows += [jnp.concatenate([pick(core, v), swap(pick(1 - core, v))], axis=1) for v in y]
    rows = jnp.concatenate(rows, axis=0)
    za_w, zb_w, own_w = (
        jnp.concatenate([v, o], axis=1)
        for v, o in ((za, swap(za)), (zb, swap(zb)), (momentum, m_o))
    )

    def chip_chunk(blocks):
        columns = jnp.concatenate(blocks, axis=0)
        return narrow(dot(rows, columns, 1, 1)).reshape(4, H, columns.shape[0])

    cut = CUT - B
    sums = [
        sum_x(chip_chunk([za_w, own_w[:cut]]), xi),
        sum_x(chip_chunk([zb_w, own_w[cut:]]), xi),
    ]
    grams = []
    for total in sums:
        part, other = gram_chunk(total, xi)
        n = part.shape[2]
        gram = jnp.zeros((4, 2, H, n), jnp.bfloat16)
        gram = lax.dynamic_update_slice(gram, part[:, None], (0, core, 0, 0))
        gram = lax.dynamic_update_slice(gram, other[:, None], (0, 1 - core, 0, 0))
        grams.append(gram.reshape(4 * B, n))

    def split(a, b, own):
        return [jnp.concatenate(v, axis=0) for v in ([a, own[:cut]], [b, own[cut:]])]

    part, backs = products(
        grams, split(za, zb, momentum), jnp.concatenate([momentum] + y, axis=0)
    )
    sent, back_a = lax.optimization_barrier((narrow(part), backs[0]))
    first = collect(part, sent, [back_a, backs[1]])
    here = narrow(first)
    rows = jnp.concatenate([here] + fetch_y(here), axis=0)
    part, backs = products(grams, split(*fetch_z(here), here), rows)
    sent, *backs = lax.optimization_barrier((narrow(part), *backs))
    second = collect(part, sent, backs)
    return narrow(coef_a * wide(momentum) + coef_b * first + coef_c * second)


def solution(mesh):
    fine = Mesh(mesh.devices.reshape(4, 4, 4, 2, 2), AXES)
    spec = P(("y", "zl"), ("x", "zh", "core"))
    return jax.shard_map(body, mesh=fine, in_specs=(spec,), out_specs=spec, check_vma=False)
```

```python
import jax
import jax.numpy as jnp
from jax import lax
from jax.sharding import Mesh, PartitionSpec as P

C = 10240
B = 336
H = 168
CUT = 512

coef_a = 3.4445
coef_b = -4.775
coef_c = 2.0315

AXES = ("y", "zl", "x", "zh", "core")
OFFSETS = (1, 2, 3)
ORDER_X = (2, 1, 3)


def send_xor(v, axis, size, k):
    return lax.ppermute(v, axis, [(i, i ^ k) for i in range(size)])


def send_up(v, axis, size, k):
    return lax.ppermute(v, axis, [(i, (i + k) % size) for i in range(size)])


def wide(v):
    return v.astype(jnp.float32)


def narrow(v):
    return v.astype(jnp.bfloat16)


def dot(a, b, da, db):
    return lax.dot_general(a, b, (((da,), (db,)), ((), ())), preferred_element_type=jnp.float32)


def swap(v):
    return send_xor(v, "core", 2, 1)


def pick(core, v):
    return jnp.where(core == 0, v[:H], v[H:])


SLOT_A = [(1, 0), (3, 1), (0, 2), (2, 3)]
SLOT_B = [(3, 0), (1, 2)]


def fetch_z(v):
    return [lax.ppermute(v, "zl", SLOT_A), lax.ppermute(v, "zl", SLOT_B)]


def fetch_y(v):
    return [send_up(v, "y", 4, -s) for s in OFFSETS]


def add(total, v):
    return lax.optimization_barrier(total + wide(v))


def apply_gram(gram, columns, rows):
    def row_block(s):
        return dot(gram[s * B : (s + 1) * B], columns, 1, 0)

    def over_y(s):
        return send_up(narrow(row_block(s)), "y", 4, s)

    def over_z(place, slot):
        back = dot(gram[:, place : place + B], rows, 0, 0)
        return lax.ppermute(narrow(back), "zl", [(b, a) for a, b in slot])

    total = add(row_block(0), over_y(2))
    total = add(total, over_z(CUT, SLOT_B))
    total = add(total, over_y(1))
    total = add(total, over_z(0, SLOT_A))
    return total + wide(over_y(3))


def sum_x(chip, xi):
    total = wide(lax.dynamic_index_in_dim(chip, xi, 0, keepdims=False))
    got = []
    for k in ORDER_X:
        piece = lax.dynamic_index_in_dim(chip, xi ^ k, 0, keepdims=False)
        got.append(send_xor(piece, "x", 4, k))
    return add(add(total, got[0]), got[1]) + wide(got[2])


def gram_chunk(total, xi):
    total = total + wide(send_xor(narrow(total), "zh", 2, 1))
    mine = narrow(total / C)
    rows = jnp.zeros((4,) + mine.shape, jnp.bfloat16)
    rows = lax.dynamic_update_index_in_dim(rows, mine, xi, 0)
    for k in ORDER_X:
        rows = lax.dynamic_update_index_in_dim(rows, send_xor(mine, "x", 4, k), xi ^ k, 0)
    return rows, swap(rows)


def body(momentum):
    core = lax.axis_index("core")
    xi = lax.axis_index("x")
    y = fetch_y(momentum)
    za, zb = fetch_z(momentum)
    later, y[0] = lax.optimization_barrier((momentum, y[0]))
    m_o = swap(later)
    rows = [jnp.concatenate([pick(core, momentum), pick(core, m_o)], axis=1)]
    rows += [jnp.concatenate([pick(core, v), swap(pick(1 - core, v))], axis=1) for v in y]
    rows = jnp.concatenate(rows, axis=0)
    za_w, zb_w, own_w = (
        jnp.concatenate([v, o], axis=1)
        for v, o in ((za, swap(za)), (zb, swap(zb)), (momentum, m_o))
    )

    def chip_chunk(blocks):
        columns = jnp.concatenate(blocks, axis=0)
        return narrow(dot(rows, columns, 1, 1)).reshape(4, H, columns.shape[0])

    cut = CUT - B
    sum_a = sum_x(chip_chunk([za_w, own_w[:cut]]), xi)
    sum_b = sum_x(chip_chunk([zb_w, own_w[cut:]]), xi)
    gram = jnp.zeros((4, 2, H, 3 * B), jnp.bfloat16)
    for total, place in ((sum_a, 0), (sum_b, CUT)):
        part, other = gram_chunk(total, xi)
        gram = lax.dynamic_update_slice(gram, part[:, None], (0, core, 0, place))
        gram = lax.dynamic_update_slice(gram, other[:, None], (0, 1 - core, 0, place))
    gram = gram.reshape(4 * B, 3 * B)
    columns = jnp.concatenate([za, momentum[:cut], zb, momentum[cut:]], axis=0)
    first = apply_gram(gram, columns, jnp.concatenate([momentum] + y, axis=0))
    sent = narrow(first)
    rows = jnp.concatenate([sent] + fetch_y(sent), axis=0)
    za, zb = fetch_z(sent)
    columns = jnp.concatenate([za, sent[:cut], zb, sent[cut:]], axis=0)
    second = apply_gram(gram, columns, rows)
    return narrow(coef_a * wide(momentum) + coef_b * first + coef_c * second)


def solution(mesh):
    fine = Mesh(mesh.devices.reshape(4, 4, 4, 2, 2), AXES)
    spec = P(("y", "zl"), ("x", "zh", "core"))
    return jax.shard_map(body, mesh=fine, in_specs=(spec,), out_specs=spec, check_vma=False)
```

```python
import jax
import jax.numpy as jnp
from jax import lax
from jax.sharding import Mesh, PartitionSpec as P

C = 10240
B = 336
H = 168
CUT = 512

coef_a = 3.4445
coef_b = -4.775
coef_c = 2.0315

AXES = ("y", "zl", "x", "zh", "core")
OFFSETS = (1, 2, 3)


def send_xor(v, axis, size, k):
    return lax.ppermute(v, axis, [(i, i ^ k) for i in range(size)])


def send_up(v, axis, size, k):
    return lax.ppermute(v, axis, [(i, (i + k) % size) for i in range(size)])


def wide(v):
    return v.astype(jnp.float32)


def narrow(v):
    return v.astype(jnp.bfloat16)


def dot(a, b, da, db):
    return lax.dot_general(a, b, (((da,), (db,)), ((), ())), preferred_element_type=jnp.float32)


def swap(v):
    return send_xor(v, "core", 2, 1)


def pick(core, v):
    return jnp.where(core == 0, v[:H], v[H:])


SLOT_A = [(1, 0), (3, 1), (0, 2), (2, 3)]
SLOT_B = [(3, 0), (1, 2)]


def fetch_z(v):
    return [lax.ppermute(v, "zl", SLOT_A), lax.ppermute(v, "zl", SLOT_B)]


def fetch_y(v):
    return [send_up(v, "y", 4, -s) for s in (1, 3, 2)]


def transposed(gram, rows):
    return narrow(dot(gram[:, : 2 * B], rows, 0, 0))


def apply_gram(gram, columns, back):
    part = dot(gram, columns, 1, 0)
    sent, back = lax.optimization_barrier((narrow(part), back))
    total = part[:B]
    total = lax.optimization_barrier(total + wide(send_up(sent[3 * B : 4 * B], "y", 4, 2)))
    total = lax.optimization_barrier(total + wide(lax.ppermute(back[:B], "zl", [(b, a) for a, b in SLOT_A])))
    total = lax.optimization_barrier(total + wide(send_up(sent[2 * B : 3 * B], "y", 4, 3)))
    total = lax.optimization_barrier(total + wide(send_up(sent[1 * B : 2 * B], "y", 4, 1)))
    total = total + wide(lax.ppermute(back[B:], "zl", [(b, a) for a, b in SLOT_B]))
    return total


def sum_x(chip, xi):
    total = wide(lax.dynamic_index_in_dim(chip, xi, 0, keepdims=False))
    for k in OFFSETS:
        piece = lax.dynamic_index_in_dim(chip, xi ^ k, 0, keepdims=False)
        total = total + wide(send_xor(piece, "x", 4, k))
    return total


def gram_chunk(total, xi):
    total = total + wide(send_xor(narrow(total), "zh", 2, 1))
    mine = narrow(total / C)
    rows = jnp.zeros((4,) + mine.shape, jnp.bfloat16)
    rows = lax.dynamic_update_index_in_dim(rows, mine, xi, 0)
    for k in OFFSETS:
        rows = lax.dynamic_update_index_in_dim(rows, send_xor(mine, "x", 4, k), xi ^ k, 0)
    return rows, swap(rows)


def body(momentum):
    core = lax.axis_index("core")
    xi = lax.axis_index("x")
    y = fetch_y(momentum)
    za, zb = fetch_z(momentum)
    m_o = swap(momentum)
    rows = [jnp.concatenate([pick(core, momentum), pick(core, m_o)], axis=1)]
    rows += [jnp.concatenate([pick(core, v), swap(pick(1 - core, v))], axis=1) for v in y]
    rows = jnp.concatenate(rows, axis=0)
    za_w, zb_w, own_w = (
        jnp.concatenate([v, o], axis=1)
        for v, o in ((za, swap(za)), (zb, swap(zb)), (momentum, m_o))
    )

    def chip_chunk(blocks):
        columns = jnp.concatenate(blocks, axis=0)
        return narrow(dot(rows, columns, 1, 1)).reshape(4, H, columns.shape[0])

    cut = CUT - B
    sum_a = sum_x(chip_chunk([za_w, zb_w[:cut]]), xi)
    sum_b = sum_x(chip_chunk([zb_w[cut:], own_w]), xi)
    gram = jnp.zeros((4, 2, H, 3 * B), jnp.bfloat16)
    for total, place in ((sum_a, 0), (sum_b, CUT)):
        part, other = gram_chunk(total, xi)
        gram = lax.dynamic_update_slice(gram, part[:, None], (0, core, 0, place))
        gram = lax.dynamic_update_slice(gram, other[:, None], (0, 1 - core, 0, place))
    gram = gram.reshape(4 * B, 3 * B)
    columns = jnp.concatenate([za, zb, momentum], axis=0)
    rows = jnp.concatenate([momentum] + y, axis=0)
    first = apply_gram(gram, columns, transposed(gram, rows))
    sent = narrow(first)
    rows = jnp.zeros((4 * B, sent.shape[1]), jnp.bfloat16)
    columns = jnp.zeros((3 * B, sent.shape[1]), jnp.bfloat16)
    rows = lax.dynamic_update_slice(rows, sent, (0, 0))
    columns = lax.dynamic_update_slice(columns, sent, (2 * B, 0))
    rows = lax.dynamic_update_slice(rows, send_up(sent, "y", 4, -2), (3 * B, 0))
    rows, columns = lax.optimization_barrier((rows, columns))
    columns = lax.dynamic_update_slice(columns, lax.ppermute(sent, "zl", SLOT_A), (0 * B, 0))
    rows, columns = lax.optimization_barrier((rows, columns))
    rows = lax.dynamic_update_slice(rows, send_up(sent, "y", 4, -3), (2 * B, 0))
    rows, columns = lax.optimization_barrier((rows, columns))
    rows = lax.dynamic_update_slice(rows, send_up(sent, "y", 4, -1), (1 * B, 0))
    back = transposed(gram, rows)
    columns, back = lax.optimization_barrier((columns, back))
    columns = lax.dynamic_update_slice(columns, lax.ppermute(sent, "zl", SLOT_B), (1 * B, 0))
    second = apply_gram(gram, columns, back)
    return narrow(coef_a * wide(momentum) + coef_b * first + coef_c * second)


def solution(mesh):
    fine = Mesh(mesh.devices.reshape(4, 4, 4, 2, 2), AXES)
    spec = P(("y", "zl"), ("x", "zh", "core"))
    return jax.shard_map(body, mesh=fine, in_specs=(spec,), out_specs=spec, check_vma=False)
```

```python
import jax
import jax.numpy as jnp
from jax import lax
from jax.sharding import Mesh, PartitionSpec as P

C = 10240
B = 336
H = 168
CUT = 512

coef_a = 3.4445
coef_b = -4.775
coef_c = 2.0315

AXES = ("y", "zl", "x", "zh", "core")
OFFSETS = (1, 2, 3)


def send_xor(v, axis, size, k):
    return lax.ppermute(v, axis, [(i, i ^ k) for i in range(size)])


def send_up(v, axis, size, k):
    return lax.ppermute(v, axis, [(i, (i + k) % size) for i in range(size)])


def wide(v):
    return v.astype(jnp.float32)


def narrow(v):
    return v.astype(jnp.bfloat16)


def dot(a, b, da, db):
    return lax.dot_general(a, b, (((da,), (db,)), ((), ())), preferred_element_type=jnp.float32)


def swap(v):
    return send_xor(v, "core", 2, 1)


def pick(core, v):
    return jnp.where(core == 0, v[:H], v[H:])


SLOT_A = [(1, 0), (3, 1), (0, 2), (2, 3)]
SLOT_B = [(3, 0), (1, 2)]


def fetch_z(v):
    return [lax.ppermute(v, "zl", SLOT_A), lax.ppermute(v, "zl", SLOT_B)]


def fetch_y(v):
    return [send_up(v, "y", 4, -s) for s in (1, 3, 2)]


def transposed(gram, rows):
    return narrow(dot(gram[:, : 2 * B], rows, 0, 0))


def apply_gram(gram, columns, back):
    part = dot(gram, columns, 1, 0)
    sent, back = lax.optimization_barrier((narrow(part), back))
    total = part[:B]
    total = lax.optimization_barrier(total + wide(send_up(sent[3 * B : 4 * B], "y", 4, 2)))
    total = lax.optimization_barrier(total + wide(lax.ppermute(back[:B], "zl", [(b, a) for a, b in SLOT_A])))
    total = lax.optimization_barrier(total + wide(send_up(sent[2 * B : 3 * B], "y", 4, 3)))
    total = lax.optimization_barrier(total + wide(send_up(sent[1 * B : 2 * B], "y", 4, 1)))
    total = total + wide(lax.ppermute(back[B:], "zl", [(b, a) for a, b in SLOT_B]))
    return total


def sum_x(chip, xi):
    total = wide(lax.dynamic_index_in_dim(chip, xi, 0, keepdims=False))
    for k in OFFSETS:
        piece = lax.dynamic_index_in_dim(chip, (xi + k) % 4, 0, keepdims=False)
        total = total + wide(send_up(piece, "x", 4, k))
    return total


def gram_chunk(total, xi):
    total = total + wide(send_xor(narrow(total), "zh", 2, 1))
    mine = narrow(total / C)
    rows = jnp.zeros((4,) + mine.shape, jnp.bfloat16)
    rows = lax.dynamic_update_index_in_dim(rows, mine, xi, 0)
    for k in OFFSETS:
        rows = lax.dynamic_update_index_in_dim(rows, send_up(mine, "x", 4, k), (xi + 4 - k) % 4, 0)
    return rows, swap(rows)


def body(momentum):
    core = lax.axis_index("core")
    xi = lax.axis_index("x")
    y = fetch_y(momentum)
    za, zb = fetch_z(momentum)
    y[2], za = lax.optimization_barrier((y[2], za))
    y[1], za = lax.optimization_barrier((y[1], za))
    y[0], y[1] = lax.optimization_barrier((y[0], y[1]))
    zb, y[0] = lax.optimization_barrier((zb, y[0]))
    m_o = swap(momentum)
    rows = [jnp.concatenate([pick(core, momentum), pick(core, m_o)], axis=1)]
    rows += [jnp.concatenate([pick(core, v), swap(pick(1 - core, v))], axis=1) for v in y]
    rows = jnp.concatenate(rows, axis=0)
    za_w, zb_w, own_w = (
        jnp.concatenate([v, o], axis=1)
        for v, o in ((za, swap(za)), (zb, swap(zb)), (momentum, m_o))
    )

    def chip_chunk(blocks):
        columns = jnp.concatenate(blocks, axis=0)
        return narrow(dot(rows, columns, 1, 1)).reshape(4, H, columns.shape[0])

    cut = CUT - B
    sum_a = sum_x(chip_chunk([za_w, zb_w[:cut]]), xi)
    sum_b = sum_x(chip_chunk([zb_w[cut:], own_w]), xi)
    gram = jnp.zeros((4, 2, H, 3 * B), jnp.bfloat16)
    for total, place in ((sum_a, 0), (sum_b, CUT)):
        part, other = gram_chunk(total, xi)
        gram = lax.dynamic_update_slice(gram, part[:, None], (0, core, 0, place))
        gram = lax.dynamic_update_slice(gram, other[:, None], (0, 1 - core, 0, place))
    gram = gram.reshape(4 * B, 3 * B)
    columns = jnp.concatenate([za, zb, momentum], axis=0)
    rows = jnp.concatenate([momentum] + y, axis=0)
    first = apply_gram(gram, columns, transposed(gram, rows))
    sent = narrow(first)
    rows = jnp.zeros((4 * B, sent.shape[1]), jnp.bfloat16)
    columns = jnp.zeros((3 * B, sent.shape[1]), jnp.bfloat16)
    rows = lax.dynamic_update_slice(rows, sent, (0, 0))
    columns = lax.dynamic_update_slice(columns, sent, (2 * B, 0))
    rows = lax.dynamic_update_slice(rows, send_up(sent, "y", 4, -2), (3 * B, 0))
    rows, columns = lax.optimization_barrier((rows, columns))
    columns = lax.dynamic_update_slice(columns, lax.ppermute(sent, "zl", SLOT_A), (0 * B, 0))
    rows, columns = lax.optimization_barrier((rows, columns))
    rows = lax.dynamic_update_slice(rows, send_up(sent, "y", 4, -3), (2 * B, 0))
    rows, columns = lax.optimization_barrier((rows, columns))
    rows = lax.dynamic_update_slice(rows, send_up(sent, "y", 4, -1), (1 * B, 0))
    back = transposed(gram, rows)
    columns, back = lax.optimization_barrier((columns, back))
    columns = lax.dynamic_update_slice(columns, lax.ppermute(sent, "zl", SLOT_B), (1 * B, 0))
    second = apply_gram(gram, columns, back)
    return narrow(coef_a * wide(momentum) + coef_b * first + coef_c * second)


def solution(mesh):
    fine = Mesh(mesh.devices.reshape(4, 4, 4, 2, 2), AXES)
    spec = P(("y", "zl"), ("x", "zh", "core"))
    return jax.shard_map(body, mesh=fine, in_specs=(spec,), out_specs=spec, check_vma=False)
```

```python
import jax
import jax.numpy as jnp
from jax import lax
from jax.sharding import Mesh, PartitionSpec as P

C = 10240
B = 336
H = 168
CUT = 512

coef_a = 3.4445
coef_b = -4.775
coef_c = 2.0315

AXES = ("y", "zl", "x", "zh", "core")
OFFSETS = (1, 2, 3)


def send_xor(v, axis, size, k):
    return lax.ppermute(v, axis, [(i, i ^ k) for i in range(size)])


def send_up(v, axis, size, k):
    return lax.ppermute(v, axis, [(i, (i + k) % size) for i in range(size)])


def wide(v):
    return v.astype(jnp.float32)


def narrow(v):
    return v.astype(jnp.bfloat16)


def dot(a, b, da, db):
    return lax.dot_general(a, b, (((da,), (db,)), ((), ())), preferred_element_type=jnp.float32)


def swap(v):
    return send_xor(v, "core", 2, 1)


def pick(core, v):
    return jnp.where(core == 0, v[:H], v[H:])


SLOT_A = [(1, 0), (3, 1), (0, 2), (2, 3)]
SLOT_B = [(3, 0), (1, 2)]


def fetch_z(v):
    return [lax.ppermute(v, "zl", SLOT_A), lax.ppermute(v, "zl", SLOT_B)]


def fetch_y(v):
    return [send_up(v, "y", 4, -s) for s in (1, 3, 2)]


def transposed(gram, rows):
    return narrow(dot(gram[:, : 2 * B], rows, 0, 0))


def apply_gram(gram, columns, back):
    part = dot(gram, columns, 1, 0)
    sent, back = lax.optimization_barrier((narrow(part), back))
    total = part[:B]
    total = lax.optimization_barrier(total + wide(send_up(sent[3 * B : 4 * B], "y", 4, 2)))
    total = lax.optimization_barrier(total + wide(lax.ppermute(back[:B], "zl", [(b, a) for a, b in SLOT_A])))
    total = lax.optimization_barrier(total + wide(send_up(sent[2 * B : 3 * B], "y", 4, 3)))
    total = lax.optimization_barrier(total + wide(send_up(sent[1 * B : 2 * B], "y", 4, 1)))
    total = total + wide(lax.ppermute(back[B:], "zl", [(b, a) for a, b in SLOT_B]))
    return total


def sum_x(chip, xi):
    total = wide(lax.dynamic_index_in_dim(chip, xi, 0, keepdims=False))
    for k in OFFSETS:
        piece = lax.dynamic_index_in_dim(chip, (xi + k) % 4, 0, keepdims=False)
        total = total + wide(send_up(piece, "x", 4, k))
    return total


def gram_chunk(total, xi):
    total = total + wide(send_xor(narrow(total), "zh", 2, 1))
    mine = narrow(total / C)
    rows = jnp.zeros((4,) + mine.shape, jnp.bfloat16)
    rows = lax.dynamic_update_index_in_dim(rows, mine, xi, 0)
    for k in OFFSETS:
        rows = lax.dynamic_update_index_in_dim(rows, send_up(mine, "x", 4, k), (xi + 4 - k) % 4, 0)
    return rows, swap(rows)


def body(momentum):
    core = lax.axis_index("core")
    xi = lax.axis_index("x")
    y = fetch_y(momentum)
    za, zb = fetch_z(momentum)
    m_o = swap(momentum)
    rows = [jnp.concatenate([pick(core, momentum), pick(core, m_o)], axis=1)]
    rows += [jnp.concatenate([pick(core, v), swap(pick(1 - core, v))], axis=1) for v in y]
    rows = jnp.concatenate(rows, axis=0)
    za_w, zb_w, own_w = (
        jnp.concatenate([v, o], axis=1)
        for v, o in ((za, swap(za)), (zb, swap(zb)), (momentum, m_o))
    )

    def chip_chunk(blocks):
        columns = jnp.concatenate(blocks, axis=0)
        return narrow(dot(rows, columns, 1, 1)).reshape(4, H, columns.shape[0])

    cut = CUT - B
    sum_a = sum_x(chip_chunk([za_w, zb_w[:cut]]), xi)
    sum_b = sum_x(chip_chunk([zb_w[cut:], own_w]), xi)
    gram = jnp.zeros((4, 2, H, 3 * B), jnp.bfloat16)
    for total, place in ((sum_a, 0), (sum_b, CUT)):
        part, other = gram_chunk(total, xi)
        gram = lax.dynamic_update_slice(gram, part[:, None], (0, core, 0, place))
        gram = lax.dynamic_update_slice(gram, other[:, None], (0, 1 - core, 0, place))
    gram = gram.reshape(4 * B, 3 * B)
    columns = jnp.concatenate([za, zb, momentum], axis=0)
    rows = jnp.concatenate([momentum] + y, axis=0)
    first = apply_gram(gram, columns, transposed(gram, rows))
    sent = narrow(first)
    rows = jnp.zeros((4 * B, sent.shape[1]), jnp.bfloat16)
    columns = jnp.zeros((3 * B, sent.shape[1]), jnp.bfloat16)
    rows = lax.dynamic_update_slice(rows, sent, (0, 0))
    columns = lax.dynamic_update_slice(columns, sent, (2 * B, 0))
    rows = lax.dynamic_update_slice(rows, send_up(sent, "y", 4, -2), (3 * B, 0))
    rows, columns = lax.optimization_barrier((rows, columns))
    columns = lax.dynamic_update_slice(columns, lax.ppermute(sent, "zl", SLOT_A), (0 * B, 0))
    rows, columns = lax.optimization_barrier((rows, columns))
    rows = lax.dynamic_update_slice(rows, send_up(sent, "y", 4, -3), (2 * B, 0))
    rows, columns = lax.optimization_barrier((rows, columns))
    rows = lax.dynamic_update_slice(rows, send_up(sent, "y", 4, -1), (1 * B, 0))
    back = transposed(gram, rows)
    columns, back = lax.optimization_barrier((columns, back))
    columns = lax.dynamic_update_slice(columns, lax.ppermute(sent, "zl", SLOT_B), (1 * B, 0))
    second = apply_gram(gram, columns, back)
    return narrow(coef_a * wide(momentum) + coef_b * first + coef_c * second)


def solution(mesh):
    fine = Mesh(mesh.devices.reshape(4, 4, 4, 2, 2), AXES)
    spec = P(("y", "zl"), ("x", "zh", "core"))
    return jax.shard_map(body, mesh=fine, in_specs=(spec,), out_specs=spec, check_vma=False)
```
